32 devices in a mesh: groups: 2 (over x), strip: 16 (over z, y, core).
Axes of the slice: x: 2, y: 2, z: 4, core: 2. Of those that a mesh axis runs over, the one named last changes fastest.
Arguments:
- x_tiles: bfloat16 [128, 2, 32, 32, 128], P(('groups', 'strip')), parts along dimension 0, may hold values from -6 to 6
- grad_out: bfloat16 [128, 2, 32, 32, 128], P(('groups', 'strip')), parts along dimension 0, may hold values from -6 to 6
- tile_pos: int32 [128], P(('groups', 'strip')), parts along dimension 0, may hold values from -1 to 3, as said below
- w_spatial: bfloat16 [9, 128, 128], replicated, may hold values from -0.1875 to 0.1875
- conv_bias: float32 [128], replicated, may hold values from -3 to 3
- w_temporal: bfloat16 [3, 128, 128], replicated, may hold values from -0.3125 to 0.3125
Outputs:
- grad_in: bfloat16 [128, 2, 32, 32, 128], P(('groups', 'strip')), parts along dimension 0
- d_spatial: float32 [18, 128, 128], P('groups'), parts along dimension 0
- d_temporal: float32 [6, 128, 128], P('groups'), parts along dimension 0
- d_bias: float32 [256], P('groups'), parts along dimension 0
The draws below stay inside these ranges and needn't reach their ends.
There are 2 independent parts, one for each index of `groups`. The reference program is written for one: setup_inputs(seed, part) draws one part's arguments, and reference() takes and returns one part's arrays. A program takes and returns all parts, laid end to end along the dimension named above; an argument that names none is the same for every part. Nothing has to cross between parts.
Inputs may be any that keep to these rules, and one draw needn't show every extreme that they name: `tile_pos`: entries d * 4 to d * 4 + 3 belong to strip d: the distinct columns of its active tiles come first, then -1. Every strip has at least one active tile and some strips are wholly active. The first entries of neighbouring strips differ by at most one.
All inputs are finite; a program needn't handle non-finite values.
Results may differ from the reference program's by a relative error of at most 0.0049.
Values may be sent and summed in bfloat16 or wider, within the bound.
A program may use at most 64 MiB of HBM per device.

```python
import jax
import jax.numpy as jnp
from jax import lax

C = 128
F = 2
P_SIZE = 32
COLS = 4
CELLS = 131072
N_STRIP = 16


def draw_tile_pos(key, part):
    key = jax.random.fold_in(key, 11)
    subkeys = jax.random.split(key, 5)
    base_load = jax.random.randint(subkeys[0], (N_STRIP,), 1, COLS // 2 + 1)
    band_start = jax.random.randint(subkeys[1], (), 0, N_STRIP)
    band_len = max(1, N_STRIP // 8)
    strip_ids = jnp.arange(N_STRIP)
    in_band = (strip_ids - band_start) % N_STRIP < band_len
    tile_loads = jnp.where(in_band, COLS, base_load)
    walk_steps = jax.random.randint(subkeys[2], (N_STRIP,), -1, 2)
    start_col = jax.random.randint(subkeys[3], (), 0, COLS)
    front_col = jnp.clip(start_col + jnp.cumsum(walk_steps), 0, COLS - 1)
    shuffled = jax.vmap(lambda k: jax.random.permutation(k, COLS))(jax.random.split(subkeys[4], N_STRIP))
    reorder = jnp.argsort((shuffled == front_col[:, None]).astype(jnp.int32), axis=1, stable=True)
    others = jnp.take_along_axis(shuffled, reorder, axis=1)[:, :COLS - 1]
    listing = jnp.concatenate([front_col[:, None], others], axis=1)
    slot_ids = jnp.arange(COLS)
    result = jnp.where(slot_ids[None, :] < tile_loads[:, None], listing, -1)
    return result.reshape(-1).astype(jnp.int32)


def levels(key, dims, cuts, least, largest):
    level, own = 1.0, jax.random.fold_in(key, 6)
    for axis_at, blocks in cuts:
        heights = jnp.exp(jax.random.uniform(jax.random.fold_in(own, axis_at), (blocks,), jnp.float32, least / len(cuts), largest / len(cuts)))
        level = level * jnp.repeat(heights, dims[axis_at] // blocks).reshape([-1 if axis == axis_at else 1 for axis in range(len(dims))])
    return level


def gaussian(rng, extent, spread, bound, shards=(), kind=jnp.bfloat16):
    drawn = jax.random.normal(rng, extent, jnp.float32) * spread
    if len(shards) > 0:
        drawn = levels(rng, extent, shards, -0.22, 0.18) * drawn
    return jnp.clip(drawn, min=-bound, max=bound).astype(kind)


def setup_inputs(seed: int = 0, part: int = 0) -> dict:
    key_of = jax.random.split(jax.random.key(seed), 7)
    part_splits = jax.random.split(jax.random.fold_in(key_of[6], part), 7)
    x_tiles = gaussian(part_splits[0], (N_STRIP * COLS, F, P_SIZE, P_SIZE, C), 1.0, 6.0, ((0, 16),))
    grad_out = gaussian(part_splits[1], (N_STRIP * COLS, F, P_SIZE, P_SIZE, C), 1.0, 6.0, ((0, 16),))
    tile_pos = draw_tile_pos(jax.random.fold_in(jax.random.fold_in(key_of[6], part), 71), part)
    w_spatial = gaussian(key_of[3], (9, C, C), (9 * C) ** -0.5, 0.1875)
    conv_bias = gaussian(key_of[4], (C,), 0.5, 3.0, (), jnp.float32)
    w_temporal = gaussian(key_of[5], (3, C, C), (3 * C) ** -0.5, 0.3125)
    return dict(x_tiles=x_tiles, grad_out=grad_out, tile_pos=tile_pos, w_spatial=w_spatial, conv_bias=conv_bias, w_temporal=w_temporal)


FORWARD = [(a, b) for a in range(3) for b in range(3)]
BACKWARD = [(2 - a, 2 - b) for a in range(3) for b in range(3)]


def silu_pair(values):
    sigmoid = jax.nn.sigmoid(values)
    return values * sigmoid, sigmoid * (1.0 + values * (1.0 - sigmoid))


def spatial_columns(padded, offsets):
    height = padded.shape[1] - 2
    pieces = [padded[:, a:a + height, b:b + height, :] for a, b in offsets]
    return jnp.concatenate(pieces, axis=-1).reshape(-1, 9 * padded.shape[-1])


def backward_terms(padded, grad_tile, spatial_stack, conv_bias, temporal_back):
    frames = grad_tile.shape[0]
    channels = grad_tile.shape[-1]
    columns = spatial_columns(padded, FORWARD)
    pre_act = jnp.dot(columns, spatial_stack, preferred_element_type=jnp.float32) + conv_bias
    activation, act_slope = silu_pair(pre_act)
    hidden = activation.astype(jnp.bfloat16).reshape(frames, -1, channels)
    grad_rows = grad_tile.reshape(frames, -1, channels)
    frame_pad = ((1, 1), (0, 0), (0, 0))
    grad_pad = jnp.pad(grad_rows, frame_pad)
    hidden_pad = jnp.pad(hidden, frame_pad)
    grad_taps = jnp.concatenate([grad_pad[2 - k:2 - k + frames] for k in range(3)], axis=-1).reshape(-1, 3 * channels)
    hidden_taps = jnp.concatenate([hidden_pad[k:k + frames] for k in range(3)], axis=-1).reshape(-1, 3 * channels)
    grad_hidden = jnp.dot(grad_taps, temporal_back, preferred_element_type=jnp.float32)
    grad_pre = (grad_hidden * act_slope).astype(jnp.bfloat16)
    temporal_term = jnp.dot(hidden_taps.T, grad_rows.reshape(-1, channels), preferred_element_type=jnp.float32)
    spatial_term = jnp.dot(columns.T, grad_pre, preferred_element_type=jnp.float32)
    bias_term = jnp.sum(lax.optimization_barrier(grad_pre).astype(jnp.float32), axis=0)
    return grad_pre.reshape(grad_tile.shape), (spatial_term, temporal_term, bias_term)


def gather_window(tile_data, slot_map, tile_row, column):
    near_slots = lax.dynamic_slice(slot_map, (tile_row, column), (3, 3))
    slot_total = tile_data.shape[0]
    picked = tile_data[jnp.clip(near_slots, 0, slot_total - 1)]
    picked = jnp.where((near_slots >= 0)[:, :, None, None, None, None], picked, jnp.zeros((), tile_data.dtype))
    frames, height, channels = tile_data.shape[1], tile_data.shape[2], tile_data.shape[4]
    joined = jnp.transpose(picked, (2, 0, 3, 1, 4, 5)).reshape(frames, 3 * height, 3 * height, channels)
    return joined[:, height - 1:2 * height + 1, height - 1:2 * height + 1, :]


def reference(x_tiles, grad_out, tile_pos, w_spatial, conv_bias, w_temporal):
    slot_total = N_STRIP * COLS
    slot_index = jnp.arange(slot_total, dtype=jnp.int32)
    strip_of = slot_index // COLS
    active = tile_pos >= 0
    column = jnp.maximum(tile_pos, 0).astype(jnp.int32)
    map_row = jnp.where(active, strip_of + 1, N_STRIP + 9).astype(jnp.int32)
    slot_map = jnp.full((N_STRIP + 2, COLS + 2), -1, jnp.int32).at[map_row, column + 1].set(slot_index, mode="drop")
    spatial_stack = w_spatial.reshape(9 * C, C)
    spatial_back = jnp.transpose(w_spatial, (0, 2, 1)).reshape(9 * C, C)
    temporal_back = jnp.transpose(w_temporal, (0, 2, 1)).reshape(3 * C, C)
    zero_tile = jnp.zeros((F, P_SIZE, P_SIZE, C), jnp.bfloat16)
    zero_sums = (jnp.zeros((9 * C, C), jnp.float32), jnp.zeros((3 * C, C), jnp.float32), jnp.zeros((C,), jnp.float32))

    def first_step(partial_value, which_slot):
        def compute(unused):
            padded = gather_window(x_tiles, slot_map, strip_of[which_slot], column[which_slot])
            return backward_terms(padded, grad_out[which_slot], spatial_stack, conv_bias, temporal_back)

        def empty_slot(unused):
            return zero_tile, zero_sums

        grad_pre, tile_terms = lax.cond(active[which_slot], compute, empty_slot, 0)
        return tuple(s + t for s, t in zip(partial_value, tile_terms)), grad_pre

    partial_value, pre_grads = lax.scan(first_step, zero_sums, slot_index)

    def second_step(which_slot):
        def compute(unused):
            padded = gather_window(pre_grads, slot_map, strip_of[which_slot], column[which_slot])
            columns = spatial_columns(padded, BACKWARD)
            tile_grad = jnp.dot(columns, spatial_back, preferred_element_type=jnp.float32).astype(jnp.bfloat16)
            return tile_grad.reshape(F, P_SIZE, P_SIZE, C)

        def empty_slot(unused):
            return zero_tile

        return lax.cond(active[which_slot], compute, empty_slot, 0)

    grad_in = lax.map(second_step, slot_index)
    scale_factor = CELLS ** -0.5
    d_spatial = (partial_value[0] * scale_factor).reshape(9, C, C)
    d_temporal = (partial_value[1] * scale_factor).reshape(3, C, C)
    d_bias = partial_value[2] * scale_factor
    return grad_in, d_spatial, d_temporal, d_bias
```

```python
import functools

import jax
import jax.numpy as jnp
from jax import lax
from jax.experimental import pallas as pl
from jax.experimental.pallas import tpu as pltpu
from jax.sharding import PartitionSpec as P

MESH = pl.DeviceIdType.MESH
F32, BF16 = jnp.float32, jnp.bfloat16
PAIRS = 8


def radices_of(size):
    found, rest = [], size
    for radix in (2, 2):
        if rest % radix == 0:
            found.append(radix)
            rest //= radix
    while rest % 4 == 0:
        found.append(4)
        rest //= 4
    if rest > 1:
        found.append(rest)
    return found


def dot_rows(a, b):
    return lax.dot_general(a, b, (((0,), (0,)), ((), ())), preferred_element_type=F32)


def kernel(size, radices, chunk, scale, x_ref, g_ref, pos_ref, ws_ref, bias_ref, wt_ref,
           out_ref, ds_ref, dt_ref, db_ref,
           wf, wb, wtt, x3, gp, gpa, ha, ga, psum, tsum, bsum, edge_x, edge_g, halo_x, halo_g,
           acc, send, total, *rest):
    n_st = len(radices)
    landing = rest[:n_st]
    esend, erecv, gsend, grecv, rsend, rrecv, asend, arecv = rest[n_st:]
    slots, frames, half, _, width, ch = x_ref.shape
    wide = 3 * ch
    me = lax.axis_index("strip")

    strides, digits, partners = [], [], []
    stride = 1
    for radix in radices:
        digit = lax.rem(me // stride, radix)
        strides.append(stride)
        digits.append(digit)
        partners.append([me + (lax.rem(digit + d, radix) - digit) * stride for d in range(1, radix)])
        stride *= radix

    barrier = pltpu.get_barrier_semaphore()
    greeted = [lax.rem(me + 1, size), lax.rem(me + size - 1, size)]
    for stage in partners:
        greeted += stage
    for other in greeted:
        pl.semaphore_signal(barrier, inc=1, device_id={"strip": other}, device_id_type=MESH)

    def slot_of(c):
        slot, act = jnp.int32(0), jnp.int32(0)
        for s in range(slots):
            hit = (pos_ref[s] == c) & (c >= 0)
            slot = jnp.where(hit, s, slot)
            act = jnp.where(hit, 1, act)
        return slot, act.astype(F32)

    def edge_copies(edge, halo, ssem, rsem):
        up = pltpu.make_async_remote_copy(
            src_ref=edge.at[0], dst_ref=halo.at[1], send_sem=ssem.at[0], recv_sem=rsem.at[1],
            device_id={"strip": jnp.maximum(me - 1, 0)}, device_id_type=MESH)
        down = pltpu.make_async_remote_copy(
            src_ref=edge.at[1], dst_ref=halo.at[0], send_sem=ssem.at[1], recv_sem=rsem.at[0],
            device_id={"strip": jnp.minimum(me + 1, size - 1)}, device_id_type=MESH)
        return up, down

    def edge_start(copies):
        up, down = copies

        @pl.when(me > 0)
        def _():
            up.start()

        @pl.when(me < size - 1)
        def _():
            down.start()

    def edge_wait(copies):
        up, down = copies

        @pl.when(me > 0)
        def _():
            up.wait_send()
            down.wait_recv()

        @pl.when(me < size - 1)
        def _():
            down.wait_send()
            up.wait_recv()

    for halo in (halo_x, halo_g):
        @pl.when(me == 0)
        def _():
            halo[0] = jnp.zeros_like(halo[0])

        @pl.when(me == size - 1)
        def _():
            halo[1] = jnp.zeros_like(halo[1])

    for c in range(slots):
        slot, act = slot_of(c)
        for f in range(frames):
            edge_x[0, c, f] = (x_ref[slot, f, 0, 0].astype(F32) * act).astype(BF16)
            edge_x[1, c, f] = (x_ref[slot, f, half - 1, 1].astype(F32) * act).astype(BF16)
    pl.semaphore_wait(barrier, len(greeted))
    x_copies = edge_copies(edge_x, halo_x, esend, erecv)
    edge_start(x_copies)

    zero = jnp.zeros((ch, ch), BF16)
    for r in range(4):
        for b in range(3):
            rows = pl.ds((r * 3 + b) * ch, ch)
            wf[rows, :ch] = ws_ref[3 * r + b] if r < 3 else zero
            wf[rows, ch:] = ws_ref[3 * (r - 1) + b] if r > 0 else zero
            if r == 3:
                wb[rows, :ch] = zero
            if r == 0:
                wb[rows, ch:] = zero
            if r < 3:
                turned = ws_ref[3 * (2 - r) + 2 - b].astype(F32).T.astype(BF16)
                wb[rows, :ch] = turned
                wb[pl.ds(((r + 1) * 3 + b) * ch, ch), ch:] = turned
    for row, col, k in ((0, 0, 1), (0, 1, 2), (1, 0, 0), (1, 1, 1)):
        wtt[row * ch:(row + 1) * ch, col * ch:(col + 1) * ch] = wt_ref[k].astype(F32).T.astype(BF16)
    psum[...] = jnp.zeros_like(psum)
    tsum[...] = jnp.zeros_like(tsum)
    bsum[...] = jnp.zeros_like(bsum)
    bias_pair = jnp.concatenate([bias_ref[...], bias_ref[...]], axis=1)

    column = lax.broadcasted_iota(jnp.int32, (1, width, 1), 1)

    def put(f, q, t, center, left, right):
        mid = center.astype(F32)
        before = jnp.where(column == 0, left, pltpu.roll(mid, 1, 1))
        after = jnp.where(column == width - 1, right, pltpu.roll(mid, width - 1, 1))
        x3[f, q, t, :, :ch] = before.astype(BF16)
        x3[f, q, t, :, ch:2 * ch] = center
        x3[f, q, t, :, 2 * ch:] = after.astype(BF16)

    def last_col(values, keep):
        return values.astype(F32)[:, -1:, :] * keep

    def first_col(values, keep):
        return values.astype(F32)[:, :1, :] * keep

    tail = slice(width - 16, width)
    head = slice(0, 16)

    def put_halo(halo, c, left_keep, right_keep):
        lc, rc = jnp.maximum(c - 1, 0), jnp.minimum(c + 1, slots - 1)
        for side, q, t in ((0, 0, 0), (1, half, 1)):
            for f in range(frames):
                put(f, pl.ds(q, 1), t, halo[side, pl.ds(c, 1), f],
                    last_col(halo[side, pl.ds(lc, 1), f, tail], left_keep),
                    first_col(halo[side, pl.ds(rc, 1), f, head], right_keep))

    def taps(f, m, r):
        part = x3[f, pl.ds(m + r // 2, PAIRS), r % 2]
        return part.reshape(PAIRS * width, wide)

    def four(f, m):
        return jnp.concatenate([taps(f, m, r) for r in range(4)], axis=1)

    span = PAIRS * width
    steps = half // PAIRS

    edge_wait(x_copies)

    def first(c, carry):
        slot, act = slot_of(c)
        lslot, lact = slot_of(c - 1)
        rslot, ract = slot_of(c + 1)
        inner_l = (c > 0).astype(F32)
        inner_r = (c < slots - 1).astype(F32)
        put_halo(halo_x, c, inner_l, inner_r)

        def build(i, carry):
            m = i * PAIRS
            for f in range(frames):
                for t in range(2):
                    rows = pl.ds(m, PAIRS)
                    put(f, pl.ds(m + t, PAIRS), 1 - t, x_ref[slot, f, rows, t],
                        last_col(x_ref[lslot, f, rows, t, tail], lact),
                        first_col(x_ref[rslot, f, rows, t, head], ract))
            return carry

        lax.fori_loop(0, steps, build, 0)

        def advance(i, carry):
            m = i * PAIRS
            rows = pl.ds(m, PAIRS)
            grads, hid = [], []
            for t in range(2):
                both = [g_ref[slot, f, rows, t].reshape(span, ch) for f in range(frames)]
                pair = jnp.concatenate(both, axis=1)
                ga[pl.ds((2 * i + t) * span, span), :] = pair
                grads.append(jnp.dot(pair, wtt[...], preferred_element_type=F32))
            for f in range(frames):
                pre = jnp.dot(four(f, m), wf[...], preferred_element_type=F32) + bias_pair
                sig = 0.5 * jnp.tanh(0.5 * pre) + 0.5
                hidden = pre * sig
                slope = sig + hidden * (1.0 - sig)
                gh = jnp.concatenate([grads[0][:, f * ch:(f + 1) * ch], grads[1][:, f * ch:(f + 1) * ch]], axis=1)
                gpre = (gh * (slope * act)).astype(BF16)
                hid_b = (hidden * act).astype(BF16)
                for t in range(2):
                    ha[pl.ds((2 * i + t) * span, span), f * ch:(f + 1) * ch] = hid_b[:, t * ch:(t + 1) * ch]
                    gp[c, f, pl.ds(m + t, PAIRS), 1 - t] = gpre[:, t * ch:(t + 1) * ch].reshape(PAIRS, width, ch)
                gpa[pl.ds((f * steps + i) * span, span), :] = gpre
                wide_g = gpre.astype(F32).reshape(span // 8, 8, 2 * ch)
                bsum[...] += jnp.sum(wide_g, axis=0)
            return carry

        lax.fori_loop(0, steps, advance, 0)
        tsum[...] += dot_rows(ha[...], ga[...])
        gpv = gpa[...]
        for r in range(4):
            cells = x3[:, pl.ds(r // 2, half), r % 2].reshape(frames * half * width, wide)
            psum[r] += dot_rows(gpv, cells)
        return carry

    lax.fori_loop(0, slots, first, 0)

    for c in range(slots):
        for f in range(frames):
            edge_g[0, c, f] = gp[c, f, 0, 1]
            edge_g[1, c, f] = gp[c, f, half, 0]
    g_copies = edge_copies(edge_g, halo_g, gsend, grecv)
    edge_start(g_copies)

    for a in range(3):
        for b in range(3):
            cols = slice(b * ch, (b + 1) * ch)
            block = psum[a, :ch, cols] + psum[a + 1, ch:, cols]
            acc[pl.ds((3 * a + b) * ch, ch), :] = block.T
    base = 9 * ch
    acc[base:base + ch, :] = tsum[:ch, ch:]
    acc[base + ch:base + 2 * ch, :] = tsum[:ch, :ch] + tsum[ch:, ch:]
    acc[base + 2 * ch:base + 3 * ch, :] = tsum[ch:, :ch]
    base = 12 * ch
    acc[base:, :] = jnp.zeros_like(acc[base:, :])
    acc[base:base + 8, :] = bsum[:, :ch] + bsum[:, ch:]

    lows, parts = [], []
    low, part = 0, size * chunk
    for radix, digit in zip(radices, digits):
        part //= radix
        lows.append(low)
        parts.append(part)
        low = low + digit * part
    own = low

    def at(offset, rows):
        return pl.ds(pl.multiple_of(offset, 16), rows)

    started = []

    def scatter_copy(k, d):
        radix, part = radices[k], parts[k]
        target = lax.rem(digits[k] + d, radix)
        return pltpu.make_async_remote_copy(
            src_ref=send.at[at(lows[k] + target * part, part)], dst_ref=landing[k].at[d - 1],
            send_sem=rsend.at[k, d], recv_sem=rrecv.at[k, d],
            device_id={"strip": partners[k][d - 1]}, device_id_type=MESH)

    def scatter_start(k):
        part = parts[k]
        for d in range(1, radices[k]):
            target = lax.rem(digits[k] + d, radices[k])
            rows = at(lows[k] + target * part, part)
            send[rows, :] = acc[rows, :].astype(BF16)
            copy = scatter_copy(k, d)
            copy.start()
            started.append(copy)

    def scatter_finish(k):
        rows = at(lows[k] + digits[k] * parts[k], parts[k])
        for d in range(1, radices[k]):
            scatter_copy(k, d).wait_recv()
        got = acc[rows, :]
        for d in range(1, radices[k]):
            got = got + landing[k][d - 1].astype(F32)
        acc[rows, :] = got

    def gather_copy(k, d, back):
        part = parts[k]
        digit = lax.rem(digits[k] + radices[k] - d, radices[k]) if back else digits[k]
        rows = at(lows[k] + digit * part, part)
        return pltpu.make_async_remote_copy(
            src_ref=total.at[rows], dst_ref=total.at[rows],
            send_sem=asend.at[k, d], recv_sem=arecv.at[k, d],
            device_id={"strip": partners[k][d - 1]}, device_id_type=MESH)

    def gather_start(k):
        for d in range(1, radices[k]):
            copy = gather_copy(k, d, False)
            copy.start()
            started.append(copy)

    def gather_finish(k):
        for d in range(1, radices[k]):
            gather_copy(k, d, True).wait_recv()

    work = [functools.partial(scatter_start, 0)]
    for k in range(n_st):
        def hop(k=k):
            scatter_finish(k)
            if k + 1 < n_st:
                scatter_start(k + 1)
            else:
                rows = at(own, chunk)
                total[rows, :] = acc[rows, :].astype(BF16)
                gather_start(n_st - 1)
        work.append(hop)
    for k in reversed(range(n_st)):
        def back(k=k):
            gather_finish(k)
            if k > 0:
                gather_start(k - 1)
        work.append(back)

    work.pop(0)()
    edge_wait(g_copies)

    for s in range(slots):
        c = jnp.maximum(pos_ref[s], 0)
        act = (pos_ref[s] >= 0).astype(F32)
        inner_l = (c > 0).astype(F32)
        inner_r = (c < slots - 1).astype(F32)
        lc, rc = jnp.maximum(c - 1, 0), jnp.minimum(c + 1, slots - 1)
        put_halo(halo_g, c, inner_l, inner_r)

        def build(i, carry):
            m = i * PAIRS
            for f in range(frames):
                for t in range(2):
                    q = pl.ds(m + t, PAIRS)
                    put(f, q, 1 - t, gp[c, f, q, 1 - t],
                        last_col(gp[lc, f, q, 1 - t, tail], inner_l),
                        first_col(gp[rc, f, q, 1 - t, head], inner_r))
            return carry

        lax.fori_loop(0, steps, build, 0)

        def second(i, carry):
            m = i * PAIRS
            for f in range(frames):
                res = (jnp.dot(four(f, m), wb[...], preferred_element_type=F32) * act).astype(BF16)
                for t in range(2):
                    out_ref[s, f, pl.ds(m, PAIRS), t] = res[:, t * ch:(t + 1) * ch].reshape(PAIRS, width, ch)
            return carry

        lax.fori_loop(0, steps, second, 0)
        work.pop(0)()
    while work:
        work.pop(0)()

    for tap in range(9):
        ds_ref[tap] = total[tap * ch:(tap + 1) * ch, :].astype(F32) * scale
    for tap in range(3):
        dt_ref[tap] = total[(9 + tap) * ch:(10 + tap) * ch, :].astype(F32) * scale
    base = 12 * ch
    rows = total[base:base + 16, :].astype(F32)
    db_ref[...] = jnp.sum(rows, axis=0, keepdims=True) * scale
    for copy in started:
        copy.wait_send()


def per_device(size, x_tiles, grad_out, tile_pos, w_spatial, conv_bias, w_temporal):
    slots, frames, height, width, ch = x_tiles.shape
    half = height // 2
    radices = radices_of(size)
    rows = 12 * ch + 16
    chunk = -(-rows // (size * 16)) * 16
    full = chunk * size
    scale = float(size * slots * frames * height * height) ** -0.5
    cells = frames * half * width
    paired = (slots, frames, half, 2, width, ch)
    edge = (2, slots, frames, width, ch)
    landing, part = [], full
    for radix in radices:
        part //= radix
        landing.append(pltpu.VMEM((radix - 1, part, ch), BF16))
    most = max(radices)
    vmem = pl.BlockSpec(memory_space=pltpu.VMEM)
    smem = pl.BlockSpec(memory_space=pltpu.SMEM)
    grad_in, d_spatial, d_temporal, d_bias = pl.pallas_call(
        functools.partial(kernel, size, radices, chunk, scale),
        out_shape=(
            jax.ShapeDtypeStruct(paired, BF16),
            jax.ShapeDtypeStruct((9, ch, ch), F32),
            jax.ShapeDtypeStruct((3, ch, ch), F32),
            jax.ShapeDtypeStruct((1, ch), F32),
        ),
        in_specs=[vmem, vmem, smem, vmem, vmem, vmem],
        out_specs=(vmem, vmem, vmem, vmem),
        scratch_shapes=[
            pltpu.VMEM((12 * ch, 2 * ch), BF16),
            pltpu.VMEM((12 * ch, 2 * ch), BF16),
            pltpu.VMEM((2 * ch, 2 * ch), BF16),
            pltpu.VMEM((frames, half + 1, 2, width, 3 * ch), BF16),
            pltpu.VMEM((slots, frames, half + 1, 2, width, ch), BF16),
            pltpu.VMEM((cells, 2 * ch), BF16),
            pltpu.VMEM((cells, 2 * ch), BF16),
            pltpu.VMEM((cells, 2 * ch), BF16),
            pltpu.VMEM((4, 2 * ch, 3 * ch), F32),
            pltpu.VMEM((2 * ch, 2 * ch), F32),
            pltpu.VMEM((8, 2 * ch), F32),
            pltpu.VMEM(edge, BF16),
            pltpu.VMEM(edge, BF16),
            pltpu.VMEM(edge, BF16),
            pltpu.VMEM(edge, BF16),
            pltpu.VMEM((full, ch), F32),
            pltpu.VMEM((full, ch), BF16),
            pltpu.VMEM((full, ch), BF16),
            *landing,
            pltpu.SemaphoreType.DMA((2,)),
            pltpu.SemaphoreType.DMA((2,)),
            pltpu.SemaphoreType.DMA((2,)),
            pltpu.SemaphoreType.DMA((2,)),
            pltpu.SemaphoreType.DMA((len(radices), most)),
            pltpu.SemaphoreType.DMA((len(radices), most)),
            pltpu.SemaphoreType.DMA((len(radices), most)),
            pltpu.SemaphoreType.DMA((len(radices), most)),
        ],
        compiler_params=pltpu.CompilerParams(
            collective_id=0, has_side_effects=True, vmem_limit_bytes=48 * 2**20
        ),
    )(
        x_tiles.reshape(paired),
        grad_out.reshape(paired),
        tile_pos,
        w_spatial,
        conv_bias.reshape(1, ch),
        w_temporal,
    )
    return grad_in.reshape(x_tiles.shape), d_spatial, d_temporal, d_bias.reshape(ch)


def solution(mesh):
    tiles = P(("groups", "strip"), None, None, None, None)
    in_specs = (tiles, tiles, P(("groups", "strip")), P(), P(), P())
    out_specs = (tiles, P("groups", None, None), P("groups", None, None), P("groups"))
    return jax.shard_map(
        functools.partial(per_device, mesh.shape["strip"]),
        mesh=mesh, in_specs=in_specs, out_specs=out_specs, check_vma=False,
    )
```

```python
import functools

import jax
import jax.numpy as jnp
from jax import lax
from jax.experimental import pallas as pl
from jax.experimental.pallas import tpu as pltpu
from jax.sharding import PartitionSpec as P

MESH = pl.DeviceIdType.MESH
F32, BF16 = jnp.float32, jnp.bfloat16
PAIRS = 8


def radices_of(size):
    found, rest = [], size
    for radix in (2, 2):
        if rest % radix == 0:
            found.append(radix)
            rest //= radix
    while rest % 4 == 0:
        found.append(4)
        rest //= 4
    if rest > 1:
        found.append(rest)
    return found


def dot_rows(a, b):
    return lax.dot_general(a, b, (((0,), (0,)), ((), ())), preferred_element_type=F32)


def kernel(size, radices, chunk, x_hbm, g_hbm, pos_ref, ws_hbm, bias_hbm, wt_hbm,
           out_ref, tot_ref, db_ref,
           x_ref, g_ref, ws_ref, bias_ref, wt_ref, in_sem, wf, wb, wtt, x3, gp, gpa, ha, ga, psum, tsum, bsum, edge_x, edge_g, halo_x, halo_g,
           acc, send, total, bstage, *rest):
    n_st = len(radices)
    landing, blanding = rest[:n_st], rest[n_st:2 * n_st]
    esend, erecv, gsend, grecv, rsend, rrecv, asend, arecv, bsend, brecv = rest[2 * n_st:]
    loads = [
        pltpu.make_async_copy(src, dst, in_sem.at[i])
        for i, (src, dst) in enumerate(
            ((x_hbm, x_ref), (ws_hbm, ws_ref), (g_hbm, g_ref), (wt_hbm, wt_ref), (bias_hbm, bias_ref)))
    ]
    for load in loads:
        load.start()
    slots, frames, half, _, width, ch = x_ref.shape
    wide = 3 * ch
    me = lax.axis_index("strip")

    strides, digits, partners = [], [], []
    stride = 1
    for radix in radices:
        digit = lax.rem(me // stride, radix)
        strides.append(stride)
        digits.append(digit)
        partners.append([me + (lax.rem(digit + d, radix) - digit) * stride for d in range(1, radix)])
        stride *= radix

    barrier = pltpu.get_barrier_semaphore()
    greeted = [lax.rem(me + 1, size), lax.rem(me + size - 1, size)]
    for stage in partners:
        greeted += stage
    for other in greeted:
        pl.semaphore_signal(barrier, inc=1, device_id={"strip": other}, device_id_type=MESH)

    def slot_of(c):
        slot, act = jnp.int32(0), jnp.int32(0)
        for s in range(slots):
            hit = (pos_ref[s] == c) & (c >= 0)
            slot = jnp.where(hit, s, slot)
            act = jnp.where(hit, 1, act)
        return slot, act.astype(F32)

    def edge_copies(edge, halo, ssem, rsem):
        up = pltpu.make_async_remote_copy(
            src_ref=edge.at[0], dst_ref=halo.at[1], send_sem=ssem.at[0], recv_sem=rsem.at[1],
            device_id={"strip": jnp.maximum(me - 1, 0)}, device_id_type=MESH)
        down = pltpu.make_async_remote_copy(
            src_ref=edge.at[1], dst_ref=halo.at[0], send_sem=ssem.at[1], recv_sem=rsem.at[0],
            device_id={"strip": jnp.minimum(me + 1, size - 1)}, device_id_type=MESH)
        return up, down

    def edge_start(copies):
        up, down = copies

        @pl.when(me > 0)
        def _():
            up.start()

        @pl.when(me < size - 1)
        def _():
            down.start()

    def edge_wait(copies):
        up, down = copies

        @pl.when(me > 0)
        def _():
            up.wait_send()
            down.wait_recv()

        @pl.when(me < size - 1)
        def _():
            down.wait_send()
            up.wait_recv()

    for halo in (halo_x, halo_g):
        @pl.when(me == 0)
        def _():
            halo[0] = jnp.zeros_like(halo[0])

        @pl.when(me == size - 1)
        def _():
            halo[1] = jnp.zeros_like(halo[1])

    loads[0].wait()
    for c in range(slots):
        slot, act = slot_of(c)
        for f in range(frames):
            edge_x[0, c, f] = (x_ref[slot, f, 0, 0].astype(F32) * act).astype(BF16)
            edge_x[1, c, f] = (x_ref[slot, f, half - 1, 1].astype(F32) * act).astype(BF16)
    pl.semaphore_wait(barrier, len(greeted))
    x_copies = edge_copies(edge_x, halo_x, esend, erecv)
    edge_start(x_copies)

    loads[1].wait()
    loads[3].wait()
    loads[4].wait()
    zero = jnp.zeros((ch, ch), BF16)
    for r in range(4):
        for b in range(3):
            rows = pl.ds((r * 3 + b) * ch, ch)
            wf[rows, :ch] = ws_ref[3 * r + b] if r < 3 else zero
            wf[rows, ch:] = ws_ref[3 * (r - 1) + b] if r > 0 else zero
            if r == 3:
                wb[rows, :ch] = zero
            if r == 0:
                wb[rows, ch:] = zero
            if r < 3:
                turned = ws_ref[3 * (2 - r) + 2 - b].astype(F32).T.astype(BF16)
                wb[rows, :ch] = turned
                wb[pl.ds(((r + 1) * 3 + b) * ch, ch), ch:] = turned
    for row, col, k in ((0, 0, 1), (0, 1, 2), (1, 0, 0), (1, 1, 1)):
        wtt[row * ch:(row + 1) * ch, col * ch:(col + 1) * ch] = wt_ref[k].astype(F32).T.astype(BF16)
    psum[...] = jnp.zeros_like(psum)
    tsum[...] = jnp.zeros_like(tsum)
    bsum[...] = jnp.zeros_like(bsum)
    bias_pair = jnp.concatenate([bias_ref[...], bias_ref[...]], axis=1)

    column = lax.broadcasted_iota(jnp.int32, (1, width, 1), 1)

    def put(n, f, q, t, center, left, right):
        mid = center.astype(F32)
        before = jnp.where(column == 0, left, pltpu.roll(mid, 1, 1))
        after = jnp.where(column == width - 1, right, pltpu.roll(mid, width - 1, 1))
        x3[n, f, q, t, :, :ch] = before.astype(BF16)
        x3[n, f, q, t, :, ch:2 * ch] = center
        x3[n, f, q, t, :, 2 * ch:] = after.astype(BF16)

    def last_col(values, keep):
        return values.astype(F32)[:, -1:, :] * keep

    def first_col(values, keep):
        return values.astype(F32)[:, :1, :] * keep

    tail = slice(width - 16, width)
    head = slice(0, 16)

    def put_halo(halo, n, c, left_keep, right_keep):
        lc, rc = jnp.maximum(c - 1, 0), jnp.minimum(c + 1, slots - 1)
        for side, q, t in ((0, 0, 0), (1, half, 1)):
            for f in range(frames):
                put(n, f, pl.ds(q, 1), t, halo[side, pl.ds(c, 1), f],
                    last_col(halo[side, pl.ds(lc, 1), f, tail], left_keep),
                    first_col(halo[side, pl.ds(rc, 1), f, head], right_keep))

    def taps(n, f, m, r):
        part = x3[n, f, pl.ds(m + r // 2, PAIRS), r % 2]
        return part.reshape(PAIRS * width, wide)

    def four(n, f, m):
        return jnp.concatenate([taps(n, f, m, r) for r in range(4)], axis=1)

    span = PAIRS * width
    steps = half // PAIRS

    edge_wait(x_copies)
    loads[2].wait()

    def first(c, carry):
        slot, act = slot_of(c)
        lslot, lact = slot_of(c - 1)
        rslot, ract = slot_of(c + 1)
        inner_l = (c > 0).astype(F32)
        inner_r = (c < slots - 1).astype(F32)
        put_halo(halo_x, c, c, inner_l, inner_r)

        def build(i, carry):
            m = i * PAIRS
            for f in range(frames):
                for t in range(2):
                    rows = pl.ds(m, PAIRS)
                    put(c, f, pl.ds(m + t, PAIRS), 1 - t, x_ref[slot, f, rows, t],
                        last_col(x_ref[lslot, f, rows, t, tail], lact),
                        first_col(x_ref[rslot, f, rows, t, head], ract))
            return carry

        lax.fori_loop(0, steps, build, 0)

        def advance(i, carry):
            m = i * PAIRS
            rows = pl.ds(m, PAIRS)
            grads, hid = [], []
            for t in range(2):
                both = [g_ref[slot, f, rows, t].reshape(span, ch) for f in range(frames)]
                pair = jnp.concatenate(both, axis=1)
                ga[pl.ds((2 * i + t) * span, span), :] = pair
                grads.append(jnp.dot(pair, wtt[...], preferred_element_type=F32))
            for f in range(frames):
                pre = jnp.dot(four(c, f, m), wf[...], preferred_element_type=F32) + bias_pair
                sig = 0.5 * jnp.tanh(0.5 * pre) + 0.5
                hidden = pre * sig
                slope = sig + hidden * (1.0 - sig)
                gh = jnp.concatenate([grads[0][:, f * ch:(f + 1) * ch], grads[1][:, f * ch:(f + 1) * ch]], axis=1)
                gpre = (gh * (slope * act)).astype(BF16)
                hid_b = (hidden * act).astype(BF16)
                for t in range(2):
                    ha[pl.ds((2 * i + t) * span, span), f * ch:(f + 1) * ch] = hid_b[:, t * ch:(t + 1) * ch]
                    gp[c, f, pl.ds(m + t, PAIRS), 1 - t] = gpre[:, t * ch:(t + 1) * ch].reshape(PAIRS, width, ch)
                gpa[c, pl.ds((f * steps + i) * span, span), :] = gpre
                wide_g = gpre.astype(F32).reshape(span // 8, 8, 2 * ch)
                bsum[...] += jnp.sum(wide_g, axis=0)
            return carry

        lax.fori_loop(0, steps, advance, 0)
        tsum[...] += dot_rows(ha[...], ga[...])
        return carry

    lax.fori_loop(0, slots, first, 0)

    for c in range(slots):
        for f in range(frames):
            edge_g[0, c, f] = gp[c, f, 0, 1]
            edge_g[1, c, f] = gp[c, f, half, 0]
    g_copies = edge_copies(edge_g, halo_g, gsend, grecv)
    edge_start(g_copies)

    def kernel_sums(taps_of):
        def add(c, carry):
            turned = gpa[c]
            for r in taps_of:
                cells = x3[c, :, pl.ds(r // 2, half), r % 2].reshape(frames * half * width, wide)
                psum[r] += dot_rows(turned, cells)
            return carry

        lax.fori_loop(0, slots, add, 0)

    def spread(piece, base, a):
        for b in range(3):
            cols = slice(b * ch, (b + 1) * ch)
            block = psum[a, :ch, cols] + psum[a + 1, ch:, cols]
            acc[piece, pl.ds(base + b * ch, ch), :] = block.T

    if size * chunk > 6 * ch:
        acc[:, 6 * ch:, :] = jnp.zeros_like(acc[:, 6 * ch:, :])
    acc[0, :ch, :] = tsum[:ch, ch:]
    acc[0, ch:2 * ch, :] = tsum[:ch, :ch] + tsum[ch:, ch:]
    acc[0, 2 * ch:3 * ch, :] = tsum[ch:, :ch]
    bstage[0] = bsum[:, :ch] + bsum[:, ch:]

    lows, parts = [], []
    low, part = 0, size * chunk
    for radix, digit in zip(radices, digits):
        part //= radix
        lows.append(low)
        parts.append(part)
        low = low + digit * part
    own = low

    def at(offset, rows):
        return pl.ds(pl.multiple_of(offset, 16), rows)

    started = []

    def scatter_copy(p, k, d):
        target = lax.rem(digits[k] + d, radices[k])
        return pltpu.make_async_remote_copy(
            src_ref=send.at[p, at(lows[k] + target * parts[k], parts[k])], dst_ref=landing[k].at[p, d - 1],
            send_sem=rsend.at[p, k, d], recv_sem=rrecv.at[p, k, d],
            device_id={"strip": partners[k][d - 1]}, device_id_type=MESH)

    def bias_copy(k, d):
        return pltpu.make_async_remote_copy(
            src_ref=bstage.at[k], dst_ref=blanding[k].at[digits[k]],
            send_sem=bsend.at[k, d], recv_sem=brecv.at[k, d],
            device_id={"strip": partners[k][d - 1]}, device_id_type=MESH)

    def go(copy):
        copy.start()
        started.append(copy)

    def scatter_start(p, k):
        for d in range(1, radices[k]):
            target = lax.rem(digits[k] + d, radices[k])
            rows = at(lows[k] + target * parts[k], parts[k])
            send[p, rows, :] = acc[p, rows, :].astype(BF16)
            go(scatter_copy(p, k, d))
        if p == 0:
            for d in range(1, radices[k]):
                go(bias_copy(k, d))
            blanding[k][digits[k]] = bstage[k]

    def scatter_finish(p, k):
        rows = at(lows[k] + digits[k] * parts[k], parts[k])
        got = acc[p, rows, :]
        for d in range(1, radices[k]):
            scatter_copy(p, k, d).wait_recv()
            got = got + landing[k][p, d - 1].astype(F32)
        acc[p, rows, :] = got
        if p == 0:
            for d in range(1, radices[k]):
                bias_copy(k, d).wait_recv()
            bstage[k + 1] = jnp.sum(blanding[k][...], axis=0)

    def gather_copy(p, k, d, back):
        digit = lax.rem(digits[k] + radices[k] - d, radices[k]) if back else digits[k]
        rows = at(lows[k] + digit * parts[k], parts[k])
        return pltpu.make_async_remote_copy(
            src_ref=total.at[p, rows], dst_ref=total.at[p, rows],
            send_sem=asend.at[p, k, d], recv_sem=arecv.at[p, k, d],
            device_id={"strip": partners[k][d - 1]}, device_id_type=MESH)

    def hop(p, k):
        scatter_finish(p, k)
        if k + 1 < n_st:
            scatter_start(p, k + 1)
        else:
            rows = at(own, chunk)
            total[p, rows, :] = acc[p, rows, :].astype(BF16)
            for d in range(1, radices[k]):
                go(gather_copy(p, k, d, False))

    def back(p, k):
        for d in range(1, radices[k]):
            gather_copy(p, k, d, True).wait_recv()
        if k > 0:
            for d in range(1, radices[k - 1]):
                go(gather_copy(p, k - 1, d, False))

    def chain(p):
        return [functools.partial(hop, p, k) for k in range(n_st)] + [
            functools.partial(back, p, k) for k in reversed(range(n_st))]

    chains = [chain(0), chain(1)]

    def run_next(p):
        if chains[p]:
            chains[p].pop(0)()

    kernel_sums((0, 1))
    spread(0, 3 * ch, 0)
    scatter_start(0, 0)
    kernel_sums((2, 3))
    run_next(0)
    spread(1, 0, 1)
    spread(1, 3 * ch, 2)
    scatter_start(1, 0)
    edge_wait(g_copies)

    for s in range(slots):
        c = jnp.maximum(pos_ref[s], 0)
        act = (pos_ref[s] >= 0).astype(F32)
        inner_l = (c > 0).astype(F32)
        inner_r = (c < slots - 1).astype(F32)
        lc, rc = jnp.maximum(c - 1, 0), jnp.minimum(c + 1, slots - 1)
        put_halo(halo_g, s, c, inner_l, inner_r)

        def build(i, carry):
            m = i * PAIRS
            for f in range(frames):
                for t in range(2):
                    q = pl.ds(m + t, PAIRS)
                    put(s, f, q, 1 - t, gp[c, f, q, 1 - t],
                        last_col(gp[lc, f, q, 1 - t, tail], inner_l),
                        first_col(gp[rc, f, q, 1 - t, head], inner_r))
            return carry

        lax.fori_loop(0, steps, build, 0)

        def second(i, carry):
            m = i * PAIRS
            for f in range(frames):
                res = (jnp.dot(four(s, f, m), wb[...], preferred_element_type=F32) * act).astype(BF16)
                for t in range(2):
                    out_ref[s, f, pl.ds(m, PAIRS), t] = res[:, t * ch:(t + 1) * ch].reshape(PAIRS, width, ch)
            return carry

        lax.fori_loop(0, steps, second, 0)
        run_next(0)
        run_next(1)
    while chains[0] or chains[1]:
        run_next(0)
        run_next(1)

    tot_ref[...] = total[:, :6 * ch, :]
    db_ref[...] = bstage[n_st]
    for copy in started:
        copy.wait_send()


def finish(scale, gi_ref, tot_ref, sum_ref, out_ref, ds_ref, dt_ref, db_ref, ds, dt, db, sems):
    ch = ds.shape[-1]
    tiles = pltpu.make_async_copy(gi_ref, out_ref, sems.at[0])
    tiles.start()
    for k in range(3):
        dt[k] = tot_ref[0, k * ch:(k + 1) * ch, :].astype(F32) * scale
        ds[k] = tot_ref[0, (3 + k) * ch:(4 + k) * ch, :].astype(F32) * scale
    for k in range(6):
        ds[3 + k] = tot_ref[1, k * ch:(k + 1) * ch, :].astype(F32) * scale
    db[...] = jnp.sum(sum_ref[...], axis=0, keepdims=True) * scale
    copies = [
        pltpu.make_async_copy(src, dst, sems.at[1 + i])
        for i, (src, dst) in enumerate(((ds, ds_ref), (dt, dt_ref), (db, db_ref)))
    ]
    for copy in copies:
        copy.start()
    for copy in copies:
        copy.wait()
    tiles.wait()


def per_device(size, x_tiles, grad_out, tile_pos, w_spatial, conv_bias, w_temporal):
    slots, frames, height, width, ch = x_tiles.shape
    half = height // 2
    radices = radices_of(size)
    rows = 6 * ch
    chunk = -(-rows // (size * 16)) * 16
    full = chunk * size
    scale = float(size * slots * frames * height * height) ** -0.5
    cells = frames * half * width
    paired = (slots, frames, half, 2, width, ch)
    edge = (2, slots, frames, width, ch)
    landing, part = [], full
    for radix in radices:
        part //= radix
        landing.append(pltpu.VMEM((2, radix - 1, part, ch), BF16))
    most = max(radices)
    vmem = pl.BlockSpec(memory_space=pltpu.VMEM)
    smem = pl.BlockSpec(memory_space=pltpu.SMEM)
    anywhere = pl.BlockSpec(memory_space=pl.ANY)
    grads, totals, bias_sum = pl.pallas_call(
        functools.partial(kernel, size, radices, chunk),
        out_shape=(
            jax.ShapeDtypeStruct(paired, BF16),
            jax.ShapeDtypeStruct((2, 6 * ch, ch), BF16),
            jax.ShapeDtypeStruct((8, ch), F32),
        ),
        in_specs=[anywhere, anywhere, smem, anywhere, anywhere, anywhere],
        out_specs=(vmem, vmem, vmem),
        scratch_shapes=[
            pltpu.VMEM(paired, BF16),
            pltpu.VMEM(paired, BF16),
            pltpu.VMEM((9, ch, ch), BF16),
            pltpu.VMEM((1, ch), F32),
            pltpu.VMEM((3, ch, ch), BF16),
            pltpu.SemaphoreType.DMA((5,)),
            pltpu.VMEM((12 * ch, 2 * ch), BF16),
            pltpu.VMEM((12 * ch, 2 * ch), BF16),
            pltpu.VMEM((2 * ch, 2 * ch), BF16),
            pltpu.VMEM((slots, frames, half + 1, 2, width, 3 * ch), BF16),
            pltpu.VMEM((slots, frames, half + 1, 2, width, ch), BF16),
            pltpu.VMEM((slots, cells, 2 * ch), BF16),
            pltpu.VMEM((cells, 2 * ch), BF16),
            pltpu.VMEM((cells, 2 * ch), BF16),
            pltpu.VMEM((4, 2 * ch, 3 * ch), F32),
            pltpu.VMEM((2 * ch, 2 * ch), F32),
            pltpu.VMEM((8, 2 * ch), F32),
            pltpu.VMEM(edge, BF16),
            pltpu.VMEM(edge, BF16),
            pltpu.VMEM(edge, BF16),
            pltpu.VMEM(edge, BF16),
            pltpu.VMEM((2, full, ch), F32),
            pltpu.VMEM((2, full, ch), BF16),
            pltpu.VMEM((2, full, ch), BF16),
            pltpu.VMEM((len(radices) + 1, 8, ch), F32),
            *landing,
            *[pltpu.VMEM((radix, 8, ch), F32) for radix in radices],
            pltpu.SemaphoreType.DMA((2,)),
            pltpu.SemaphoreType.DMA((2,)),
            pltpu.SemaphoreType.DMA((2,)),
            pltpu.SemaphoreType.DMA((2,)),
            pltpu.SemaphoreType.DMA((2, len(radices), most)),
            pltpu.SemaphoreType.DMA((2, len(radices), most)),
            pltpu.SemaphoreType.DMA((2, len(radices), most)),
            pltpu.SemaphoreType.DMA((2, len(radices), most)),
            pltpu.SemaphoreType.DMA((len(radices), most)),
            pltpu.SemaphoreType.DMA((len(radices), most)),
        ],
        compiler_params=pltpu.CompilerParams(
            collective_id=0, has_side_effects=True, vmem_limit_bytes=48 * 2**20
        ),
    )(
        x_tiles.reshape(paired),
        grad_out.reshape(paired),
        tile_pos,
        w_spatial,
        conv_bias.reshape(1, ch),
        w_temporal,
    )
    grad_in, d_spatial, d_temporal, d_bias = pl.pallas_call(
        functools.partial(finish, scale),
        out_shape=(
            jax.ShapeDtypeStruct(paired, BF16),
            jax.ShapeDtypeStruct((9, ch, ch), F32),
            jax.ShapeDtypeStruct((3, ch, ch), F32),
            jax.ShapeDtypeStruct((1, ch), F32),
        ),
        in_specs=[anywhere, vmem, vmem],
        out_specs=(anywhere, anywhere, anywhere, anywhere),
        scratch_shapes=[
            pltpu.VMEM((9, ch, ch), F32),
            pltpu.VMEM((3, ch, ch), F32),
            pltpu.VMEM((1, ch), F32),
            pltpu.SemaphoreType.DMA((4,)),
        ],
    )(grads, totals, bias_sum)
    return grad_in.reshape(x_tiles.shape), d_spatial, d_temporal, d_bias.reshape(ch)


def solution(mesh):
    tiles = P(("groups", "strip"), None, None, None, None)
    in_specs = (tiles, tiles, P(("groups", "strip")), P(), P(), P())
    out_specs = (tiles, P("groups", None, None), P("groups", None, None), P("groups"))
    return jax.shard_map(
        functools.partial(per_device, mesh.shape["strip"]),
        mesh=mesh, in_specs=in_specs, out_specs=out_specs, check_vma=False,
    )
```

```python
import functools

import jax
import jax.numpy as jnp
from jax import lax
from jax.experimental import pallas as pl
from jax.experimental.pallas import tpu as pltpu
from jax.sharding import PartitionSpec as P

MESH = pl.DeviceIdType.MESH
F32, BF16 = jnp.float32, jnp.bfloat16
PAIRS = 16


def radices_of(size):
    found, rest = [], size
    while rest % 4 == 0:
        found.append(4)
        rest //= 4
    if rest > 1:
        found.append(rest)
    return found


def dot_rows(a, b):
    return lax.dot_general(a, b, (((0,), (0,)), ((), ())), preferred_element_type=F32)


def kernel(size, radices, chunk, x_hbm, g_hbm, pos_ref, ws_hbm, bias_hbm, wt_hbm,
           out_ref, ds_ref, dt_ref, db_ref,
           x_ref, g_ref, ws_ref, bias_ref, wt_ref, in_sem, wf, wb, wtt, x3, gp, gpa, ha, ga, psum, tsum, bsum, edge_x, edge_g, halo_x, halo_g,
           acc, send, total, bstage, *rest):
    n_st = len(radices)
    landing, blanding = rest[:n_st], rest[n_st:2 * n_st]
    esend, erecv, gsend, grecv, rsend, rrecv, asend, arecv, bsend, brecv = rest[2 * n_st:]
    loads = [
        pltpu.make_async_copy(src, dst, in_sem.at[i])
        for i, (src, dst) in enumerate(
            ((x_hbm, x_ref), (ws_hbm, ws_ref), (g_hbm, g_ref), (wt_hbm, wt_ref), (bias_hbm, bias_ref)))
    ]
    for load in loads:
        load.start()
    slots, frames, half, _, width, ch = x_ref.shape
    wide = 3 * ch
    me = lax.axis_index("strip")

    strides, digits, partners = [], [], []
    stride = 1
    for radix in radices:
        digit = lax.rem(me // stride, radix)
        strides.append(stride)
        digits.append(digit)
        partners.append([me + (lax.rem(digit + d, radix) - digit) * stride for d in range(1, radix)])
        stride *= radix

    barrier = pltpu.get_barrier_semaphore()
    greeted = [lax.rem(me + 1, size), lax.rem(me + size - 1, size)]
    for stage in partners:
        greeted += stage
    for other in greeted:
        pl.semaphore_signal(barrier, inc=1, device_id={"strip": other}, device_id_type=MESH)

    def slot_of(c):
        slot, act = jnp.int32(0), jnp.int32(0)
        for s in range(slots):
            hit = (pos_ref[s] == c) & (c >= 0)
            slot = jnp.where(hit, s, slot)
            act = jnp.where(hit, 1, act)
        return slot, act.astype(F32)

    def edge_copies(edge, halo, ssem, rsem):
        up = pltpu.make_async_remote_copy(
            src_ref=edge.at[0], dst_ref=halo.at[1], send_sem=ssem.at[0], recv_sem=rsem.at[1],
            device_id={"strip": jnp.maximum(me - 1, 0)}, device_id_type=MESH)
        down = pltpu.make_async_remote_copy(
            src_ref=edge.at[1], dst_ref=halo.at[0], send_sem=ssem.at[1], recv_sem=rsem.at[0],
            device_id={"strip": jnp.minimum(me + 1, size - 1)}, device_id_type=MESH)
        return up, down

    def edge_start(copies):
        up, down = copies

        @pl.when(me > 0)
        def _():
            up.start()

        @pl.when(me < size - 1)
        def _():
            down.start()

    def edge_wait(copies):
        up, down = copies

        @pl.when(me > 0)
        def _():
            up.wait_send()
            down.wait_recv()

        @pl.when(me < size - 1)
        def _():
            down.wait_send()
            up.wait_recv()

    for halo in (halo_x, halo_g):
        @pl.when(me == 0)
        def _():
            halo[0] = jnp.zeros_like(halo[0])

        @pl.when(me == size - 1)
        def _():
            halo[1] = jnp.zeros_like(halo[1])

    loads[0].wait()
    for c in range(slots):
        slot, act = slot_of(c)
        for f in range(frames):
            edge_x[0, c, f] = (x_ref[slot, f, 0, 0].astype(F32) * act).astype(BF16)
            edge_x[1, c, f] = (x_ref[slot, f, half - 1, 1].astype(F32) * act).astype(BF16)
    pl.semaphore_wait(barrier, len(greeted))
    x_copies = edge_copies(edge_x, halo_x, esend, erecv)
    edge_start(x_copies)

    loads[1].wait()
    loads[3].wait()
    loads[4].wait()
    zero = jnp.zeros((ch, ch), BF16)
    for r in range(4):
        for b in range(3):
            rows = pl.ds((r * 3 + b) * ch, ch)
            wf[rows, :ch] = ws_ref[3 * r + b] if r < 3 else zero
            wf[rows, ch:] = ws_ref[3 * (r - 1) + b] if r > 0 else zero
            if r == 3:
                wb[rows, :ch] = zero
            if r == 0:
                wb[rows, ch:] = zero
            if r < 3:
                turned = ws_ref[3 * (2 - r) + 2 - b].astype(F32).T.astype(BF16)
                wb[rows, :ch] = turned
                wb[pl.ds(((r + 1) * 3 + b) * ch, ch), ch:] = turned
    for row, col, k in ((0, 0, 1), (0, 1, 2), (1, 0, 0), (1, 1, 1)):
        wtt[row * ch:(row + 1) * ch, col * ch:(col + 1) * ch] = wt_ref[k].astype(F32).T.astype(BF16)
    psum[...] = jnp.zeros_like(psum)
    tsum[...] = jnp.zeros_like(tsum)
    bsum[...] = jnp.zeros_like(bsum)
    bias_pair = jnp.concatenate([bias_ref[...], bias_ref[...]], axis=1)

    column = lax.broadcasted_iota(jnp.int32, (1, width, 1), 1)

    def put(n, f, q, t, center, left, right):
        mid = center.astype(F32)
        before = jnp.where(column == 0, left, pltpu.roll(mid, 1, 1))
        after = jnp.where(column == width - 1, right, pltpu.roll(mid, width - 1, 1))
        x3[n, f, q, t, :, :ch] = before.astype(BF16)
        x3[n, f, q, t, :, ch:2 * ch] = center
        x3[n, f, q, t, :, 2 * ch:] = after.astype(BF16)

    def last_col(values, keep):
        return values.astype(F32)[:, -1:, :] * keep

    def first_col(values, keep):
        return values.astype(F32)[:, :1, :] * keep

    tail = slice(width - 16, width)
    head = slice(0, 16)

    def put_halo(halo, n, c, left_keep, right_keep):
        lc, rc = jnp.maximum(c - 1, 0), jnp.minimum(c + 1, slots - 1)
        for side, q, t in ((0, 0, 0), (1, half, 1)):
            for f in range(frames):
                put(n, f, pl.ds(q, 1), t, halo[side, pl.ds(c, 1), f],
                    last_col(halo[side, pl.ds(lc, 1), f, tail], left_keep),
                    first_col(halo[side, pl.ds(rc, 1), f, head], right_keep))

    def taps(n, f, m, r):
        part = x3[n, f, pl.ds(m + r // 2, PAIRS), r % 2]
        return part.reshape(PAIRS * width, wide)

    def four(n, f, m):
        return jnp.concatenate([taps(n, f, m, r) for r in range(4)], axis=1)

    span = PAIRS * width
    steps = half // PAIRS

    edge_wait(x_copies)
    loads[2].wait()

    def first(c, carry):
        slot, act = slot_of(c)
        lslot, lact = slot_of(c - 1)
        rslot, ract = slot_of(c + 1)
        inner_l = (c > 0).astype(F32)
        inner_r = (c < slots - 1).astype(F32)
        put_halo(halo_x, c, c, inner_l, inner_r)

        def build(i, carry):
            m = i * PAIRS
            for f in range(frames):
                for t in range(2):
                    rows = pl.ds(m, PAIRS)
                    put(c, f, pl.ds(m + t, PAIRS), 1 - t, x_ref[slot, f, rows, t],
                        last_col(x_ref[lslot, f, rows, t, tail], lact),
                        first_col(x_ref[rslot, f, rows, t, head], ract))
            return carry

        lax.fori_loop(0, steps, build, 0)

        def advance(i, carry):
            m = i * PAIRS
            rows = pl.ds(m, PAIRS)
            grads, hid = [], []
            for t in range(2):
                both = [g_ref[slot, f, rows, t].reshape(span, ch) for f in range(frames)]
                pair = jnp.concatenate(both, axis=1)
                ga[pl.ds((2 * i + t) * span, span), :] = pair
                grads.append(jnp.dot(pair, wtt[...], preferred_element_type=F32))
            for f in range(frames):
                pre = jnp.dot(four(c, f, m), wf[...], preferred_element_type=F32) + bias_pair
                sig = 0.5 * jnp.tanh(0.5 * pre) + 0.5
                hidden = pre * sig
                slope = sig + hidden * (1.0 - sig)
                gh = jnp.concatenate([grads[0][:, f * ch:(f + 1) * ch], grads[1][:, f * ch:(f + 1) * ch]], axis=1)
                gpre = (gh * (slope * act)).astype(BF16)
                hid_b = (hidden * act).astype(BF16)
                for t in range(2):
                    ha[pl.ds((2 * i + t) * span, span), f * ch:(f + 1) * ch] = hid_b[:, t * ch:(t + 1) * ch]
                    gp[c, f, pl.ds(m + t, PAIRS), 1 - t] = gpre[:, t * ch:(t + 1) * ch].reshape(PAIRS, width, ch)
                gpa[c, pl.ds((f * steps + i) * span, span), :] = gpre
                wide_g = gpre.astype(F32).reshape(span // 8, 8, 2 * ch)
                bsum[...] += jnp.sum(wide_g, axis=0)
            return carry

        lax.fori_loop(0, steps, advance, 0)
        tsum[...] += dot_rows(ha[...], ga[...])
        return carry

    lax.fori_loop(0, slots, first, 0)

    for c in range(slots):
        for f in range(frames):
            edge_g[0, c, f] = gp[c, f, 0, 1]
            edge_g[1, c, f] = gp[c, f, half, 0]
    g_copies = edge_copies(edge_g, halo_g, gsend, grecv)
    edge_start(g_copies)

    def kernel_sums(taps_of):
        def add(c, carry):
            turned = gpa[c]
            for r in taps_of:
                cells = x3[c, :, pl.ds(r // 2, half), r % 2].reshape(frames * half * width, wide)
                psum[r] += dot_rows(turned, cells)
            return carry

        lax.fori_loop(0, slots, add, 0)

    def spread(piece, base, a):
        for b in range(3):
            cols = slice(b * ch, (b + 1) * ch)
            block = psum[a, :ch, cols] + psum[a + 1, ch:, cols]
            acc[piece, pl.ds(base + b * ch, ch), :] = block.T

    if size * chunk > 6 * ch:
        acc[:, 6 * ch:, :] = jnp.zeros_like(acc[:, 6 * ch:, :])
    acc[0, :ch, :] = tsum[:ch, ch:]
    acc[0, ch:2 * ch, :] = tsum[:ch, :ch] + tsum[ch:, ch:]
    acc[0, 2 * ch:3 * ch, :] = tsum[ch:, :ch]
    bstage[0] = bsum[:, :ch] + bsum[:, ch:]

    lows, parts = [], []
    low, part = 0, size * chunk
    for radix, digit in zip(radices, digits):
        part //= radix
        lows.append(low)
        parts.append(part)
        low = low + digit * part
    own = low

    def at(offset, rows):
        return pl.ds(pl.multiple_of(offset, 16), rows)

    started = []

    def scatter_copy(p, k, d):
        target = lax.rem(digits[k] + d, radices[k])
        return pltpu.make_async_remote_copy(
            src_ref=send.at[p, at(lows[k] + target * parts[k], parts[k])], dst_ref=landing[k].at[p, d - 1],
            send_sem=rsend.at[p, k, d], recv_sem=rrecv.at[p, k, d],
            device_id={"strip": partners[k][d - 1]}, device_id_type=MESH)

    def bias_copy(k, d):
        return pltpu.make_async_remote_copy(
            src_ref=bstage.at[k], dst_ref=blanding[k].at[digits[k]],
            send_sem=bsend.at[k, d], recv_sem=brecv.at[k, d],
            device_id={"strip": partners[k][d - 1]}, device_id_type=MESH)

    def go(copy):
        copy.start()
        started.append(copy)

    def scatter_start(p, k):
        for d in range(1, radices[k]):
            target = lax.rem(digits[k] + d, radices[k])
            rows = at(lows[k] + target * parts[k], parts[k])
            send[p, rows, :] = acc[p, rows, :].astype(BF16)
            go(scatter_copy(p, k, d))
        if p == 0:
            for d in range(1, radices[k]):
                go(bias_copy(k, d))
            blanding[k][digits[k]] = bstage[k]

    def scatter_finish(p, k):
        rows = at(lows[k] + digits[k] * parts[k], parts[k])
        got = acc[p, rows, :]
        for d in range(1, radices[k]):
            scatter_copy(p, k, d).wait_recv()
            got = got + landing[k][p, d - 1].astype(F32)
        acc[p, rows, :] = got
        if p == 0:
            for d in range(1, radices[k]):
                bias_copy(k, d).wait_recv()
            bstage[k + 1] = jnp.sum(blanding[k][...], axis=0)

    def gather_copy(p, k, d, back):
        digit = lax.rem(digits[k] + radices[k] - d, radices[k]) if back else digits[k]
        rows = at(lows[k] + digit * parts[k], parts[k])
        return pltpu.make_async_remote_copy(
            src_ref=total.at[p, rows], dst_ref=total.at[p, rows],
            send_sem=asend.at[p, k, d], recv_sem=arecv.at[p, k, d],
            device_id={"strip": partners[k][d - 1]}, device_id_type=MESH)

    def hop(p, k):
        scatter_finish(p, k)
        if k + 1 < n_st:
            scatter_start(p, k + 1)
        else:
            rows = at(own, chunk)
            total[p, rows, :] = acc[p, rows, :].astype(BF16)
            for d in range(1, radices[k]):
                go(gather_copy(p, k, d, False))

    def back(p, k):
        for d in range(1, radices[k]):
            gather_copy(p, k, d, True).wait_recv()
        if k > 0:
            for d in range(1, radices[k - 1]):
                go(gather_copy(p, k - 1, d, False))

    def chain(p):
        return [functools.partial(hop, p, k) for k in range(n_st)] + [
            functools.partial(back, p, k) for k in reversed(range(n_st))]

    chains = [chain(0), chain(1)]

    def run_next(p):
        if chains[p]:
            chains[p].pop(0)()

    kernel_sums((0, 1))
    spread(0, 3 * ch, 0)
    scatter_start(0, 0)
    kernel_sums((2, 3))
    spread(1, 0, 1)
    spread(1, 3 * ch, 2)
    scatter_start(1, 0)
    run_next(0)
    edge_wait(g_copies)

    for s in range(slots):
        c = jnp.maximum(pos_ref[s], 0)
        act = (pos_ref[s] >= 0).astype(F32)
        inner_l = (c > 0).astype(F32)
        inner_r = (c < slots - 1).astype(F32)
        lc, rc = jnp.maximum(c - 1, 0), jnp.minimum(c + 1, slots - 1)
        put_halo(halo_g, s, c, inner_l, inner_r)

        def build(i, carry):
            m = i * PAIRS
            for f in range(frames):
                for t in range(2):
                    q = pl.ds(m + t, PAIRS)
                    put(s, f, q, 1 - t, gp[c, f, q, 1 - t],
                        last_col(gp[lc, f, q, 1 - t, tail], inner_l),
                        first_col(gp[rc, f, q, 1 - t, head], inner_r))
            return carry

        lax.fori_loop(0, steps, build, 0)

        def second(i, carry):
            m = i * PAIRS
            for f in range(frames):
                res = (jnp.dot(four(s, f, m), wb[...], preferred_element_type=F32) * act).astype(BF16)
                for t in range(2):
                    out_ref[s, f, pl.ds(m, PAIRS), t] = res[:, t * ch:(t + 1) * ch].reshape(PAIRS, width, ch)
            return carry

        lax.fori_loop(0, steps, second, 0)
        run_next(0)
        run_next(1)
    while chains[0] or chains[1]:
        run_next(0)
        run_next(1)

    for k in range(3):
        dt_ref[k] = total[0, k * ch:(k + 1) * ch, :]
        ds_ref[k] = total[0, (3 + k) * ch:(4 + k) * ch, :]
    for k in range(6):
        ds_ref[3 + k] = total[1, k * ch:(k + 1) * ch, :]
    db_ref[...] = bstage[n_st]
    for copy in started:
        copy.wait_send()


def per_device(size, x_tiles, grad_out, tile_pos, w_spatial, conv_bias, w_temporal):
    slots, frames, height, width, ch = x_tiles.shape
    half = height // 2
    radices = radices_of(size)
    rows = 6 * ch
    chunk = -(-rows // (size * 16)) * 16
    full = chunk * size
    scale = float(size * slots * frames * height * height) ** -0.5
    cells = frames * half * width
    paired = (slots, frames, half, 2, width, ch)
    edge = (2, slots, frames, width, ch)
    landing, part = [], full
    for radix in radices:
        part //= radix
        landing.append(pltpu.VMEM((2, radix - 1, part, ch), BF16))
    most = max(radices)
    vmem = pl.BlockSpec(memory_space=pltpu.VMEM)
    smem = pl.BlockSpec(memory_space=pltpu.SMEM)
    hbm = pl.BlockSpec(memory_space=pltpu.HBM)
    grads, d_spatial, d_temporal, bias_sum = pl.pallas_call(
        functools.partial(kernel, size, radices, chunk),
        out_shape=(
            jax.ShapeDtypeStruct(paired, BF16),
            jax.ShapeDtypeStruct((9, ch, ch), BF16),
            jax.ShapeDtypeStruct((3, ch, ch), BF16),
            jax.ShapeDtypeStruct((8, ch), F32),
        ),
        in_specs=[hbm, hbm, smem, hbm, hbm, hbm],
        out_specs=(vmem, vmem, vmem, vmem),
        scratch_shapes=[
            pltpu.VMEM(paired, BF16),
            pltpu.VMEM(paired, BF16),
            pltpu.VMEM((9, ch, ch), BF16),
            pltpu.VMEM((1, ch), F32),
            pltpu.VMEM((3, ch, ch), BF16),
            pltpu.SemaphoreType.DMA((5,)),
            pltpu.VMEM((12 * ch, 2 * ch), BF16),
            pltpu.VMEM((12 * ch, 2 * ch), BF16),
            pltpu.VMEM((2 * ch, 2 * ch), BF16),
            pltpu.VMEM((slots, frames, half + 1, 2, width, 3 * ch), BF16),
            pltpu.VMEM((slots, frames, half + 1, 2, width, ch), BF16),
            pltpu.VMEM((slots, cells, 2 * ch), BF16),
            pltpu.VMEM((cells, 2 * ch), BF16),
            pltpu.VMEM((cells, 2 * ch), BF16),
            pltpu.VMEM((4, 2 * ch, 3 * ch), F32),
            pltpu.VMEM((2 * ch, 2 * ch), F32),
            pltpu.VMEM((8, 2 * ch), F32),
            pltpu.VMEM(edge, BF16),
            pltpu.VMEM(edge, BF16),
            pltpu.VMEM(edge, BF16),
            pltpu.VMEM(edge, BF16),
            pltpu.VMEM((2, full, ch), F32),
            pltpu.VMEM((2, full, ch), BF16),
            pltpu.VMEM((2, full, ch), BF16),
            pltpu.VMEM((len(radices) + 1, 8, ch), F32),
            *landing,
            *[pltpu.VMEM((radix, 8, ch), F32) for radix in radices],
            pltpu.SemaphoreType.DMA((2,)),
            pltpu.SemaphoreType.DMA((2,)),
            pltpu.SemaphoreType.DMA((2,)),
            pltpu.SemaphoreType.DMA((2,)),
            pltpu.SemaphoreType.DMA((2, len(radices), most)),
            pltpu.SemaphoreType.DMA((2, len(radices), most)),
            pltpu.SemaphoreType.DMA((2, len(radices), most)),
            pltpu.SemaphoreType.DMA((2, len(radices), most)),
            pltpu.SemaphoreType.DMA((len(radices), most)),
            pltpu.SemaphoreType.DMA((len(radices), most)),
        ],
        compiler_params=pltpu.CompilerParams(
            collective_id=0, has_side_effects=True, vmem_limit_bytes=48 * 2**20
        ),
    )(
        x_tiles.reshape(paired),
        grad_out.reshape(paired),
        tile_pos,
        w_spatial,
        conv_bias.reshape(1, ch),
        w_temporal,
    )
    d_spatial = d_spatial.astype(F32) * scale
    d_temporal = d_temporal.astype(F32) * scale
    d_bias = jnp.sum(bias_sum, axis=0) * scale
    return grads.reshape(x_tiles.shape), d_spatial, d_temporal, d_bias


def solution(mesh):
    tiles = P(("groups", "strip"), None, None, None, None)
    in_specs = (tiles, tiles, P(("groups", "strip")), P(), P(), P())
    out_specs = (tiles, P("groups", None, None), P("groups", None, None), P("groups"))
    return jax.shard_map(
        functools.partial(per_device, mesh.shape["strip"]),
        mesh=mesh, in_specs=in_specs, out_specs=out_specs, check_vma=False,
    )
```
